32 devices in a mesh: samp: 8 (over y, x, core), head: 4 (over z).
Axes of the slice: x: 2, y: 2, z: 4, core: 2. Of those that a mesh axis runs over, the one named last changes fastest.
Arguments:
- input_tokens: bfloat16 [16, 512, 768], P('samp'), may hold values from -6 to 6
- output_cotangent: bfloat16 [16, 512, 768], P('samp'), may hold values from -15 to 15
- query_weight: bfloat16 [768, 768], P(None, 'head'), may hold values from -0.21875 to 0.21875
- key_weight: bfloat16 [768, 768], P(None, 'head'), may hold values from -0.21875 to 0.21875
- value_weight: bfloat16 [768, 768], P(None, 'head'), may hold values from -0.21875 to 0.21875
- output_weight: bfloat16 [768, 768], P('head'), may hold values from -0.21875 to 0.21875
- pair_bias: bfloat16 [16, 512, 512], P('head'), may hold values from -6 to 240
- valid_len: int32 [1], replicated, may hold values from 256 to 512
- pair_in: bfloat16 [512, 512, 128], P('head', 'samp'), may hold values from -6 to 6
- w_bias: bfloat16 [128, 16], replicated, may hold values from -6 to 6
- t_gate: bfloat16 [2, 128, 256], replicated, may hold values from -0.5 to 0.5
- t_up: bfloat16 [2, 128, 256], replicated, may hold values from -0.5 to 0.5
- t_down: bfloat16 [2, 256, 128], replicated, may hold values from -0.375 to 0.375
Outputs:
- d_tokens: bfloat16 [16, 512, 768], P('samp', None, 'head')
- d_pair: bfloat16 [512, 512, 128], P('head', 'samp')
- d_trans_gate: float32 [2, 128, 256], replicated
- d_trans_up: float32 [2, 128, 256], replicated
- d_trans_down: float32 [2, 256, 128], replicated
The draws below stay inside these ranges and needn't reach their ends.
All inputs are finite; a program needn't handle non-finite values.
Results may differ from the reference program's by a relative error of at most 0.02.
Values may be sent and summed in bfloat16 or wider, within the bound.
A program may use at most 128 MiB of HBM per device.

```python
import math
import jax
import jax.numpy as jnp
from jax import lax

D = 768
HEADS = 16
HD = 48
CZ = 128
FF = 256
LAYERS = 2
TOKENS = 512
SAMP_DEV = 2
SAMPLES = 16
N_HEAD = 4


def draw_pair_bias(key, part):
    key_base = jax.random.fold_in(jax.random.fold_in(key, 7), 0)
    full_shape = (HEADS, TOKENS, TOKENS)
    bias_field = jnp.clip(jax.random.normal(key_base, full_shape, jnp.float32), -6.0, 6.0)
    return bias_field.astype(jnp.bfloat16)


def level_of(key, shape, shards, least, high):
    gain = 1.0
    for dim, blocks in shards:
        heights = jax.random.uniform(jax.random.fold_in(jax.random.fold_in(key, 6), dim), (blocks,), jnp.float32, least / len(shards), high / len(shards))
        gain = gain * jnp.repeat(jnp.exp(heights), shape[dim] // blocks).reshape((-1,) + (1,) * (len(shape) - 1 - dim))
    return gain


def scatter_about(rng, extent, width, bound, pieces=(), held_as=jnp.bfloat16):
    drawn = width * jax.random.normal(rng, extent, jnp.float32)
    if pieces:
        drawn = drawn * level_of(rng, extent, pieces, -0.22, 0.18)
    return jnp.clip(drawn, -bound, bound).astype(held_as)


def setup_inputs(seed: int = 0) -> dict:
    key_of = jax.random.split(jax.random.key(seed), 14)
    return {
        "input_tokens": scatter_about(key_of[0], (SAMPLES, TOKENS, D), 1.0, 6.0, ((0, 8),)),
        "output_cotangent": scatter_about(key_of[1], (SAMPLES, TOKENS, D), 2.5, 15.0, ((0, 8),)),
        "query_weight": scatter_about(key_of[2], (D, D), D ** -0.5, 0.21875, ((1, 4),)),
        "key_weight": scatter_about(key_of[3], (D, D), D ** -0.5, 0.21875, ((1, 4),)),
        "value_weight": scatter_about(key_of[4], (D, D), D ** -0.5, 0.21875, ((1, 4),)),
        "output_weight": scatter_about(key_of[5], (D, D), D ** -0.5, 0.21875, ((0, 4),)),
        "pair_bias": draw_pair_bias(jax.random.fold_in(key_of[13], 71), 0),
        "valid_len": jax.random.randint(key_of[7], (1,), TOKENS // 2, TOKENS + 1).astype(jnp.int32),
        "pair_in": scatter_about(key_of[8], (TOKENS, TOKENS, CZ), 1.0, 6.0, ((0, 4), (1, 8))),
        "w_bias": scatter_about(key_of[9], (CZ, HEADS), 1.0, 6.0),
        "t_gate": scatter_about(key_of[10], (LAYERS, CZ, FF), CZ ** -0.5, 0.5),
        "t_up": scatter_about(key_of[11], (LAYERS, CZ, FF), CZ ** -0.5, 0.5),
        "t_down": scatter_about(key_of[12], (LAYERS, FF, CZ), FF ** -0.5, 0.375),
    }


EPS_NORM = 1e-05
MASKED = -1e+30

def layer_forward(field, gate_weight, up_weight, down_weight):
    centred = field - lax.optimization_barrier(jnp.mean(field, axis=-1, keepdims=True))
    variance = lax.optimization_barrier(jnp.mean(centred * centred, axis=-1, keepdims=True))
    inv_std = lax.rsqrt(variance + EPS_NORM)
    normed = centred * inv_std
    normed_low = normed.astype(jnp.bfloat16)
    gate_proj = jnp.dot(normed_low, gate_weight, preferred_element_type=jnp.float32)
    up_proj = jnp.dot(normed_low, up_weight, preferred_element_type=jnp.float32)
    sigmoid_gate = jax.nn.sigmoid(gate_proj)
    hidden = (gate_proj * sigmoid_gate * up_proj).astype(jnp.bfloat16)
    result = field + jnp.dot(hidden, down_weight, preferred_element_type=jnp.float32)
    return (result, (normed, normed_low, inv_std, gate_proj, up_proj, sigmoid_gate, hidden))

def layer_backward(grad_next, saved, gate_weight, up_weight, down_weight):
    normed, normed_low, inv_std, gate_proj, up_proj, sigmoid_gate, hidden = saved
    grad_low = grad_next.astype(jnp.bfloat16)
    down_sum = jnp.dot(hidden.T, grad_low, preferred_element_type=jnp.float32)
    grad_hidden = jnp.dot(grad_low, down_weight.T, preferred_element_type=jnp.float32)
    grad_gate = (grad_hidden * up_proj * sigmoid_gate * (1.0 + gate_proj * (1.0 - sigmoid_gate))).astype(jnp.bfloat16)
    grad_up = (grad_hidden * gate_proj * sigmoid_gate).astype(jnp.bfloat16)
    gate_sum = jnp.dot(normed_low.T, grad_gate, preferred_element_type=jnp.float32)
    up_sum = jnp.dot(normed_low.T, grad_up, preferred_element_type=jnp.float32)
    grad_normed = jnp.dot(grad_gate, gate_weight.T, preferred_element_type=jnp.float32) + jnp.dot(grad_up, up_weight.T, preferred_element_type=jnp.float32)
    inner = inv_std * (grad_normed - lax.optimization_barrier(jnp.mean(grad_normed, axis=-1, keepdims=True)) - normed * lax.optimization_barrier(jnp.mean(grad_normed * normed, axis=-1, keepdims=True)))
    return (grad_next + inner, gate_sum, up_sum, down_sum)

def pair_block(pair_low, grad_top, t_gate, t_up, t_down):
    field = pair_low.astype(jnp.float32)
    saved_list = []
    for layer in range(t_gate.shape[0]):
        field, saved = layer_forward(field, t_gate[layer], t_up[layer], t_down[layer])
        saved_list.append(saved)
    grad_field = grad_top
    gate_list, up_list, down_list = ([], [], [])
    for layer in reversed(range(t_gate.shape[0])):
        grad_field, gate_sum, up_sum, down_sum = layer_backward(grad_field, saved_list[layer], t_gate[layer], t_up[layer], t_down[layer])
        gate_list.insert(0, gate_sum)
        up_list.insert(0, up_sum)
        down_list.insert(0, down_sum)
    return (grad_field, jnp.stack(gate_list), jnp.stack(up_list), jnp.stack(down_list))

def attend(query, keys, values, grad_out, bias_block, kept_keys):
    score_scale = 1.0 / math.sqrt(HD)
    query_f = query.astype(jnp.float32)
    keys_f = keys.astype(jnp.float32)
    values_f = values.astype(jnp.float32)
    grad_f = grad_out.astype(jnp.float32)
    scores = jnp.einsum('sie,sje->sij', query_f, keys_f) * score_scale + bias_block.astype(jnp.float32)[None]
    scores = jnp.where(kept_keys[None, None, :], scores, MASKED)
    row_max = lax.optimization_barrier(jnp.max(scores, axis=-1, keepdims=True))
    exp_scores = jnp.exp(scores - row_max)
    attn_probs = exp_scores / lax.optimization_barrier(jnp.sum(exp_scores, axis=-1, keepdims=True))
    probs_low = attn_probs.astype(jnp.bfloat16)
    grad_probs = jnp.einsum('sie,sje->sij', grad_f, values_f)
    grad_scores = attn_probs * (grad_probs - lax.optimization_barrier(jnp.sum(attn_probs * grad_probs, axis=-1, keepdims=True)))
    scores_low = grad_scores.astype(jnp.bfloat16).astype(jnp.float32)
    value_partial_gradient = lax.optimization_barrier(jnp.sum(grad_scores, axis=0))
    grad_query = (jnp.einsum('sij,sje->sie', scores_low, keys_f) * score_scale).astype(jnp.bfloat16)
    grad_key = (jnp.einsum('sij,sie->sje', scores_low, query_f) * score_scale).astype(jnp.bfloat16)
    grad_value = jnp.einsum('sij,sie->sje', probs_low.astype(jnp.float32), grad_f).astype(jnp.bfloat16)
    return (grad_query, grad_key, grad_value, value_partial_gradient)

def reference(input_tokens, output_cotangent, query_weight, key_weight, value_weight, output_weight, pair_bias, valid_len, pair_in, w_bias, t_gate, t_up, t_down):
    kept_keys = jnp.arange(TOKENS, dtype=jnp.int32) < valid_len[0]
    groups = SAMPLES // SAMP_DEV
    per_group = HEADS // N_HEAD
    tokens_wide_float = input_tokens.astype(jnp.float32)
    query_every_sample = jnp.einsum('tvz,zl->tvl', tokens_wide_float, query_weight.astype(jnp.float32)).astype(jnp.bfloat16)
    key_every_sample = jnp.einsum('tvz,zl->tvl', tokens_wide_float, key_weight.astype(jnp.float32)).astype(jnp.bfloat16)
    value_every_sample = jnp.einsum('tvz,zl->tvl', tokens_wide_float, value_weight.astype(jnp.float32)).astype(jnp.bfloat16)
    attention_every_sample = jnp.einsum('cjy,hy->cjh', output_cotangent.astype(jnp.float32), output_weight.astype(jnp.float32)).astype(jnp.bfloat16)

    def head_fn(head_idx):
        start = head_idx * HD

        def pick_head(array):
            return lax.dynamic_slice_in_dim(array, start, HD, 2).reshape(groups, SAMP_DEV, TOKENS, HD)
        bias_block = lax.dynamic_index_in_dim(pair_bias, head_idx, 0, keepdims=False)

        def group_fn(inputs):
            grad_query, grad_key, grad_value, value_partial_gradient = attend(inputs[0], inputs[1], inputs[2], inputs[3], bias_block, kept_keys)
            return (grad_query, grad_key, grad_value, value_partial_gradient.astype(jnp.bfloat16))
        head_outs = lax.map(group_fn, (pick_head(query_every_sample), pick_head(key_every_sample), pick_head(value_every_sample), pick_head(attention_every_sample)))
        bias_sum = lax.optimization_barrier(jnp.sum(lax.optimization_barrier(head_outs[3]).astype(jnp.float32), axis=0)).astype(jnp.bfloat16)
        return (head_outs[0].reshape(SAMPLES, TOKENS, HD), head_outs[1].reshape(SAMPLES, TOKENS, HD), head_outs[2].reshape(SAMPLES, TOKENS, HD), bias_sum)
    grad_query, grad_key, grad_value, d_bias = lax.map(head_fn, jnp.arange(HEADS, dtype=jnp.int32))

    def token_step(running, group_idx):
        first = group_idx * per_group

        def gather_group(array):
            picked = lax.dynamic_slice_in_dim(array, first, per_group, 0)
            return picked.transpose(1, 2, 0, 3).reshape(SAMPLES, TOKENS, per_group * HD)

        def weight_group(weight):
            return lax.dynamic_slice_in_dim(weight, first * HD, per_group * HD, 1)
        joined_gradients = jnp.concatenate([gather_group(grad_query), gather_group(grad_key), gather_group(grad_value)], axis=2).astype(jnp.float32)
        joined_weights = jnp.concatenate([weight_group(query_weight), weight_group(key_weight), weight_group(value_weight)], axis=1).astype(jnp.float32)
        value_partial_gradient = jnp.einsum('tla,ua->tlu', joined_gradients, joined_weights)
        rounded = lax.optimization_barrier(value_partial_gradient.astype(jnp.bfloat16)).astype(jnp.float32)
        return (running + rounded, None)
    running, _ = lax.scan(token_step, jnp.zeros((SAMPLES, TOKENS, D), jnp.float32), jnp.arange(N_HEAD, dtype=jnp.int32))
    d_tokens = running.astype(jnp.bfloat16)
    block_rows = TOKENS // N_HEAD

    def pair_step(carry, block_idx):
        start = block_idx * block_rows
        pair_rows = lax.dynamic_slice_in_dim(pair_in, start, block_rows, 0)
        bias_rows = lax.dynamic_slice_in_dim(d_bias, start, block_rows, 1)
        grad_top = jnp.einsum('hrc,zh->rcz', bias_rows.astype(jnp.float32), w_bias.astype(jnp.float32))
        grad_field, gate_sum, up_sum, down_sum = pair_block(pair_rows.reshape(block_rows * TOKENS, CZ), grad_top.reshape(block_rows * TOKENS, CZ), t_gate, t_up, t_down)
        new_carry = (carry[0] + gate_sum, carry[1] + up_sum, carry[2] + down_sum)
        return (new_carry, grad_field.reshape(block_rows, TOKENS, CZ).astype(jnp.bfloat16))
    init = (jnp.zeros(t_gate.shape, jnp.float32), jnp.zeros(t_up.shape, jnp.float32), jnp.zeros(t_down.shape, jnp.float32))
    sums, pair_blocks = lax.scan(pair_step, init, jnp.arange(N_HEAD, dtype=jnp.int32))
    d_pair = pair_blocks.reshape(TOKENS, TOKENS, CZ)
    return (d_tokens, d_pair, sums[0] / TOKENS, sums[1] / TOKENS, sums[2] / TOKENS)
```

```python
import functools
import math

import jax
import jax.numpy as jnp
from jax import lax
from jax.experimental import pallas as pl
from jax.experimental.pallas import tpu as pltpu
from jax.sharding import PartitionSpec as P

HD = 48
LANES = 128

EPS_NORM = 1e-05
MASKED = -1e30
VMEM_LIMIT = 56 * 1024 * 1024
MESH = pl.DeviceIdType.MESH


def dot(lhs, rhs, lhs_dim=1, rhs_dim=0):
    return lax.dot_general(
        lhs, rhs, (((lhs_dim,), (rhs_dim,)), ((), ())), preferred_element_type=jnp.float32
    )


def attention_kernel(
    rows,
    valid_ref,
    tokens_ref,
    cotangent_ref,
    wq_ref,
    wk_ref,
    wv_ref,
    wo_ref,
    spread_ref,
    bias_ref,
    terms_ref,
    part_ref,
    wide_in,
    wide_out,
    projected,
    attn_grad,
    joined,
    key_sum,
    value_sum,
    bias_sum,
):
    step = pl.program_id(0)
    heads, tokens, _ = bias_ref.shape
    width = heads * LANES
    scale = 1.0 / math.sqrt(HD)

    @pl.when(step == 0)
    def _():
        spread = spread_ref[...]
        for which, ref in enumerate((wq_ref, wk_ref, wv_ref)):
            wide_in[:, which * width : (which + 1) * width] = dot(ref[...], spread).astype(
                jnp.bfloat16
            )
        wide_out[...] = dot(spread, wo_ref[...], 0, 0).astype(jnp.bfloat16)
        bias_sum[...] = jnp.zeros_like(bias_sum)

    projected[...] = dot(tokens_ref[0], wide_in[...]).astype(jnp.bfloat16)
    attn_grad[...] = dot(cotangent_ref[0], wide_out[...], 1, 1).astype(jnp.bfloat16)
    kept = lax.broadcasted_iota(jnp.int32, (1, tokens), 1) < valid_ref[0]

    for head in range(heads):
        q_cols = slice(head * LANES, (head + 1) * LANES)
        k_cols = slice(width + head * LANES, width + (head + 1) * LANES)
        v_cols = slice(2 * width + head * LANES, 2 * width + (head + 1) * LANES)
        keys = projected[:, k_cols]
        values = projected[:, v_cols]
        for block in range(tokens // rows):
            span = slice(block * rows, (block + 1) * rows)
            query = projected[span, q_cols]
            grad_out = attn_grad[span, q_cols]
            scores = dot(query, keys, 1, 1) * scale + bias_ref[head, span].astype(jnp.float32)
            scores = jnp.where(kept, scores, MASKED)
            exp_scores = jnp.exp(scores - jnp.max(scores, axis=-1, keepdims=True))
            probs = exp_scores * (1.0 / jnp.sum(exp_scores, axis=-1, keepdims=True))
            grad_probs = dot(grad_out, values, 1, 1)
            delta = jnp.sum(probs * grad_probs, axis=-1, keepdims=True)
            grad_scores = probs * (grad_probs - delta)
            scores_low = grad_scores.astype(jnp.bfloat16)
            bias_sum[head, span] += grad_scores
            joined[span, q_cols] = (dot(scores_low, keys) * scale).astype(jnp.bfloat16)
            key_term = dot(scores_low, query, 0, 0)
            value_term = dot(probs.astype(jnp.bfloat16), grad_out, 0, 0)
            if block == 0:
                key_sum[...] = key_term
                value_sum[...] = value_term
            else:
                key_sum[...] += key_term
                value_sum[...] += value_term
        joined[:, k_cols] = (key_sum[...] * scale).astype(jnp.bfloat16)
        joined[:, v_cols] = value_sum[...].astype(jnp.bfloat16)

    terms_ref[0] = dot(joined[...], wide_in[...], 1, 1).astype(jnp.bfloat16)

    @pl.when(step == pl.num_programs(0) - 1)
    def _():
        part_ref[...] = bias_sum[...].astype(jnp.bfloat16)


def attention(tokens_in, cotangent, wq, wk, wv, wo, bias, valid_len):
    samples, tokens, features = tokens_in.shape
    heads = bias.shape[0]
    width = heads * LANES
    source = lax.broadcasted_iota(jnp.int32, (heads * HD, width), 0)
    place = lax.broadcasted_iota(jnp.int32, (heads * HD, width), 1)
    spread = (place == (source // HD) * LANES + source % HD).astype(jnp.bfloat16)
    vmem = pl.BlockSpec(memory_space=pltpu.VMEM)
    per_sample = pl.BlockSpec((1, tokens, features), lambda s: (s, 0, 0))
    whole_bias = pl.BlockSpec(bias.shape, lambda s: (0, 0, 0))
    return pl.pallas_call(
        functools.partial(attention_kernel, min(128, tokens)),
        grid=(samples,),
        in_specs=[pl.BlockSpec(memory_space=pltpu.SMEM), per_sample, per_sample]
        + [vmem] * 6,
        out_specs=[per_sample, whole_bias],
        out_shape=[
            jax.ShapeDtypeStruct(tokens_in.shape, jnp.bfloat16),
            jax.ShapeDtypeStruct(bias.shape, jnp.bfloat16),
        ],
        scratch_shapes=[
            pltpu.VMEM((features, 3 * width), jnp.bfloat16),
            pltpu.VMEM((width, features), jnp.bfloat16),
            pltpu.VMEM((tokens, 3 * width), jnp.bfloat16),
            pltpu.VMEM((tokens, width), jnp.bfloat16),
            pltpu.VMEM((tokens, 3 * width), jnp.bfloat16),
            pltpu.VMEM((tokens, LANES), jnp.float32),
            pltpu.VMEM((tokens, LANES), jnp.float32),
            pltpu.VMEM(bias.shape, jnp.float32),
        ],
        compiler_params=pltpu.CompilerParams(vmem_limit_bytes=VMEM_LIMIT),
        name="attention",
    )(valid_len, tokens_in, cotangent, wq, wk, wv, wo, spread, bias)


def pair_kernel(
    pair_ref, bias_ref, wb_ref, tg_ref, tu_ref, td_ref, dpair_ref, sums_ref, totals
):
    step = pl.program_id(0)
    layers, channels, _ = tg_ref.shape

    @pl.when(step == 0)
    def _():
        totals[...] = jnp.zeros_like(totals)

    field = pair_ref[...].astype(jnp.float32)
    saved = []
    for layer in range(layers):
        centred = field - jnp.mean(field, axis=-1, keepdims=True)
        variance = jnp.mean(centred * centred, axis=-1, keepdims=True)
        inv_std = lax.rsqrt(variance + EPS_NORM)
        normed = centred * inv_std
        low = normed.astype(jnp.bfloat16)
        gate = dot(low, tg_ref[layer])
        up = dot(low, tu_ref[layer])
        sig = 0.5 * jnp.tanh(0.5 * gate) + 0.5
        act = gate * sig
        hidden = (act * up).astype(jnp.bfloat16)
        saved.append((normed, low, inv_std, gate, up, sig, act, hidden))
        if layer + 1 < layers:
            field = field + dot(hidden, td_ref[layer])
    grad = dot(bias_ref[...], wb_ref[...], 0, 0)
    for layer in reversed(range(layers)):
        normed, low, inv_std, gate, up, sig, act, hidden = saved[layer]
        grad_low = grad.astype(jnp.bfloat16)
        grad_hidden = dot(grad_low, td_ref[layer], 1, 1)
        grad_gate = (grad_hidden * up * (sig + act * (1.0 - sig))).astype(jnp.bfloat16)
        grad_up = (grad_hidden * act).astype(jnp.bfloat16)
        for which, term in enumerate(
            (dot(low, grad_gate, 0, 0), dot(low, grad_up, 0, 0), dot(grad_low, hidden, 0, 0))
        ):
            first = (which * layers + layer) * channels
            totals[first : first + channels] += term
        grad_normed = dot(grad_gate, tg_ref[layer], 1, 1) + dot(grad_up, tu_ref[layer], 1, 1)
        grad = grad + inv_std * (
            grad_normed
            - jnp.mean(grad_normed, axis=-1, keepdims=True)
            - normed * jnp.mean(grad_normed * normed, axis=-1, keepdims=True)
        )
    dpair_ref[...] = grad.astype(jnp.bfloat16)

    @pl.when(step == pl.num_programs(0) - 1)
    def _():
        sums_ref[...] = totals[...].astype(jnp.bfloat16)


def pair_transitions(pair, bias_grad, w_bias, t_gate, t_up, t_down):
    pairs, channels = pair.shape
    heads = bias_grad.shape[0]
    layers, _, hidden = t_gate.shape
    tile = math.gcd(pairs, 1024)
    vmem = pl.BlockSpec(memory_space=pltpu.VMEM)
    sums = (3 * layers * channels, hidden)
    return pl.pallas_call(
        pair_kernel,
        grid=(pairs // tile,),
        in_specs=[
            pl.BlockSpec((tile, channels), lambda i: (i, 0)),
            pl.BlockSpec((heads, tile), lambda i: (0, i)),
        ]
        + [vmem] * 4,
        out_specs=[
            pl.BlockSpec((tile, channels), lambda i: (i, 0)),
            pl.BlockSpec(sums, lambda i: (0, 0)),
        ],
        out_shape=[
            jax.ShapeDtypeStruct(pair.shape, jnp.bfloat16),
            jax.ShapeDtypeStruct(sums, jnp.bfloat16),
        ],
        scratch_shapes=[pltpu.VMEM(sums, jnp.float32)],
        compiler_params=pltpu.CompilerParams(vmem_limit_bytes=VMEM_LIMIT),
        name="pair_transitions",
    )(pair, bias_grad, w_bias.T, t_gate, t_up, t_down)


def sum_kernel(
    groups,
    heads,
    divisor,
    part_ref,
    total_ref,
    landed,
    crossed,
    gathered,
    send_a,
    recv_a,
    send_b,
    recv_b,
    send_c,
    recv_c,
):
    samp, head = lax.axis_index("samp"), lax.axis_index("head")
    rows = gathered.shape[1]
    barrier = pltpu.get_barrier_semaphore()
    for k in range(1, groups):
        other = (lax.rem(samp + k, groups), head)
        pl.semaphore_signal(barrier, inc=1, device_id=other, device_id_type=MESH)
    for k in range(1, heads):
        other = (samp, lax.rem(head + k, heads))
        pl.semaphore_signal(barrier, inc=1, device_id=other, device_id_type=MESH)
    pl.semaphore_wait(barrier, groups - 1 + heads - 1)

    def piece(index):
        return pl.ds(pl.multiple_of(index * rows, 16), rows)

    scatter = []
    for k in range(1, groups):
        other = lax.rem(samp + k, groups)
        copy = pltpu.make_async_remote_copy(
            src_ref=part_ref.at[piece(other)],
            dst_ref=landed.at[k],
            send_sem=send_a.at[k],
            recv_sem=recv_a.at[k],
            device_id=(other, head),
            device_id_type=MESH,
        )
        copy.start()
        scatter.append(copy)
    running = part_ref[piece(samp)].astype(jnp.float32)
    for k, copy in enumerate(scatter):
        copy.wait_recv()
        running = running + landed[k + 1].astype(jnp.float32)
    crossed[head] = running.astype(jnp.bfloat16)
    cross = []
    for k in range(1, heads):
        copy = pltpu.make_async_remote_copy(
            src_ref=crossed.at[head],
            dst_ref=crossed.at[head],
            send_sem=send_b.at[k],
            recv_sem=recv_b.at[k],
            device_id=(samp, lax.rem(head + k, heads)),
            device_id_type=MESH,
        )
        copy.start()
        cross.append(copy)
    for copy in cross:
        copy.wait_recv()
    running = crossed[0].astype(jnp.float32)
    for k in range(1, heads):
        running = running + crossed[k].astype(jnp.float32)
    gathered[samp] = running.astype(jnp.bfloat16)
    gather = []
    for k in range(1, groups):
        copy = pltpu.make_async_remote_copy(
            src_ref=gathered.at[samp],
            dst_ref=gathered.at[samp],
            send_sem=send_c.at[k],
            recv_sem=recv_c.at[k],
            device_id=(lax.rem(samp + k, groups), head),
            device_id_type=MESH,
        )
        copy.start()
        gather.append(copy)
    for copy in gather:
        copy.wait_recv()
    for k in range(groups):
        total_ref[k] = gathered[k].astype(jnp.float32) / divisor
    for copy in scatter + cross + gather:
        copy.wait_send()


def sum_everywhere(part, groups, heads, divisor):
    size, width = part.shape
    rows = size // groups
    vmem = pl.BlockSpec(memory_space=pltpu.VMEM)
    return pl.pallas_call(
        functools.partial(sum_kernel, groups, heads, divisor),
        in_specs=[vmem],
        out_specs=vmem,
        out_shape=jax.ShapeDtypeStruct((groups, rows, width), jnp.float32),
        scratch_shapes=[
            pltpu.VMEM((groups, rows, width), jnp.bfloat16),
            pltpu.VMEM((heads, rows, width), jnp.bfloat16),
            pltpu.VMEM((groups, rows, width), jnp.bfloat16),
        ]
        + [pltpu.SemaphoreType.DMA((n,)) for n in (groups, groups, heads, heads, groups, groups)],
        compiler_params=pltpu.CompilerParams(
            collective_id=0, has_side_effects=True, vmem_limit_bytes=VMEM_LIMIT
        ),
        name="sum_everywhere",
    )(part).reshape(size, width)


def per_device(
    groups,
    head_groups,
    input_tokens,
    output_cotangent,
    query_weight,
    key_weight,
    value_weight,
    output_weight,
    pair_bias,
    valid_len,
    pair_in,
    w_bias,
    t_gate,
    t_up,
    t_down,
):
    tokens = input_tokens.shape[1]
    token_terms, bias_parts = attention(
        input_tokens,
        output_cotangent,
        query_weight,
        key_weight,
        value_weight,
        output_weight,
        pair_bias,
        valid_len,
    )
    d_tokens = lax.psum_scatter(token_terms, "head", scatter_dimension=2, tiled=True)
    summed = lax.psum_scatter(bias_parts, "samp", scatter_dimension=2, tiled=True)
    owned_grad = lax.all_to_all(summed, "head", split_axis=1, concat_axis=0, tiled=True)
    pair_rows, pair_cols, channels = pair_in.shape
    d_pair, sums = pair_transitions(
        pair_in.reshape(pair_rows * pair_cols, channels),
        owned_grad.reshape(owned_grad.shape[0], pair_rows * pair_cols),
        w_bias,
        t_gate,
        t_up,
        t_down,
    )
    totals = sum_everywhere(sums, groups, head_groups, tokens)
    layers, _, hidden = t_gate.shape
    totals = totals.reshape(3, layers, channels, hidden)
    return (
        d_tokens,
        d_pair.reshape(pair_in.shape),
        totals[0],
        totals[1],
        totals[2].transpose(0, 2, 1),
    )


def solution(mesh):
    placed = (
        P("samp", None, None),
        P("samp", None, None),
        P(None, "head"),
        P(None, "head"),
        P(None, "head"),
        P("head", None),
        P("head", None, None),
        P(),
        P("head", "samp", None),
        P(),
        P(),
        P(),
        P(),
    )
    return jax.shard_map(
        functools.partial(per_device, mesh.shape["samp"], mesh.shape["head"]),
        mesh=mesh,
        in_specs=placed,
        out_specs=(P("samp", None, "head"), P("head", "samp", None), P(), P(), P()),
        check_vma=False,
    )
```

```python
import functools
import math

import jax
import jax.numpy as jnp
from jax import lax
from jax.experimental import pallas as pl
from jax.experimental.pallas import tpu as pltpu
from jax.sharding import PartitionSpec as P

HD = 48
LANES = 128

EPS_NORM = 1e-05
MASKED = -1e30
VMEM_LIMIT = 56 * 1024 * 1024
MESH = pl.DeviceIdType.MESH


def dot(lhs, rhs, lhs_dim=1, rhs_dim=0):
    return lax.dot_general(
        lhs, rhs, (((lhs_dim,), (rhs_dim,)), ((), ())), preferred_element_type=jnp.float32
    )


def attention_kernel(
    rows,
    valid_ref,
    tokens_ref,
    cotangent_ref,
    wq_ref,
    wk_ref,
    wv_ref,
    wo_ref,
    spread_ref,
    bias_ref,
    terms_ref,
    part_ref,
    wide_in,
    wide_out,
    projected,
    attn_grad,
    joined,
    key_sum,
    value_sum,
    bias_sum,
):
    step = pl.program_id(0)
    heads, tokens, _ = bias_ref.shape
    width = heads * LANES
    scale = 1.0 / math.sqrt(HD)

    @pl.when(step == 0)
    def _():
        spread = spread_ref[...]
        for which, ref in enumerate((wq_ref, wk_ref, wv_ref)):
            wide_in[:, which * width : (which + 1) * width] = dot(ref[...], spread).astype(
                jnp.bfloat16
            )
        wide_out[...] = dot(spread, wo_ref[...], 0, 0).astype(jnp.bfloat16)
        bias_sum[...] = jnp.zeros_like(bias_sum)

    projected[...] = dot(tokens_ref[0], wide_in[...]).astype(jnp.bfloat16)
    attn_grad[...] = dot(cotangent_ref[0], wide_out[...], 1, 1).astype(jnp.bfloat16)
    kept = lax.broadcasted_iota(jnp.int32, (1, tokens), 1) < valid_ref[0]

    for head in range(heads):
        q_cols = slice(head * LANES, (head + 1) * LANES)
        k_cols = slice(width + head * LANES, width + (head + 1) * LANES)
        v_cols = slice(2 * width + head * LANES, 2 * width + (head + 1) * LANES)
        keys = projected[:, k_cols]
        values = projected[:, v_cols]
        for block in range(tokens // rows):
            span = slice(block * rows, (block + 1) * rows)
            query = projected[span, q_cols]
            grad_out = attn_grad[span, q_cols]
            scores = dot(query, keys, 1, 1) * scale + bias_ref[head, span].astype(jnp.float32)
            scores = jnp.where(kept, scores, MASKED)
            exp_scores = jnp.exp(scores - jnp.max(scores, axis=-1, keepdims=True))
            probs = exp_scores * (1.0 / jnp.sum(exp_scores, axis=-1, keepdims=True))
            grad_probs = dot(grad_out, values, 1, 1)
            delta = jnp.sum(probs * grad_probs, axis=-1, keepdims=True)
            grad_scores = probs * (grad_probs - delta)
            scores_low = grad_scores.astype(jnp.bfloat16)
            bias_sum[head, span] += grad_scores
            joined[span, q_cols] = (dot(scores_low, keys) * scale).astype(jnp.bfloat16)
            key_term = dot(scores_low, query, 0, 0)
            value_term = dot(probs.astype(jnp.bfloat16), grad_out, 0, 0)
            if block == 0:
                key_sum[...] = key_term
                value_sum[...] = value_term
            else:
                key_sum[...] += key_term
                value_sum[...] += value_term
        joined[:, k_cols] = (key_sum[...] * scale).astype(jnp.bfloat16)
        joined[:, v_cols] = value_sum[...].astype(jnp.bfloat16)

    terms_ref[0] = dot(wide_in[...], joined[...], 1, 1).astype(jnp.bfloat16)

    @pl.when(step == pl.num_programs(0) - 1)
    def _():
        for head in range(heads):
            part_ref[head] = bias_sum[head].T.astype(jnp.bfloat16)


def attention(tokens_in, cotangent, wq, wk, wv, wo, bias, valid_len):
    samples, tokens, features = tokens_in.shape
    heads = bias.shape[0]
    width = heads * LANES
    source = lax.broadcasted_iota(jnp.int32, (heads * HD, width), 0)
    place = lax.broadcasted_iota(jnp.int32, (heads * HD, width), 1)
    spread = (place == (source // HD) * LANES + source % HD).astype(jnp.bfloat16)
    vmem = pl.BlockSpec(memory_space=pltpu.VMEM)
    per_sample = pl.BlockSpec((1, tokens, features), lambda s: (s, 0, 0))
    whole_bias = pl.BlockSpec(bias.shape, lambda s: (0, 0, 0))
    return pl.pallas_call(
        functools.partial(attention_kernel, min(128, tokens)),
        grid=(samples,),
        in_specs=[pl.BlockSpec(memory_space=pltpu.SMEM), per_sample, per_sample]
        + [vmem] * 6,
        out_specs=[pl.BlockSpec((1, features, tokens), lambda s: (s, 0, 0)), whole_bias],
        out_shape=[
            jax.ShapeDtypeStruct((samples, features, tokens), jnp.bfloat16),
            jax.ShapeDtypeStruct(bias.shape, jnp.bfloat16),
        ],
        scratch_shapes=[
            pltpu.VMEM((features, 3 * width), jnp.bfloat16),
            pltpu.VMEM((width, features), jnp.bfloat16),
            pltpu.VMEM((tokens, 3 * width), jnp.bfloat16),
            pltpu.VMEM((tokens, width), jnp.bfloat16),
            pltpu.VMEM((tokens, 3 * width), jnp.bfloat16),
            pltpu.VMEM((tokens, LANES), jnp.float32),
            pltpu.VMEM((tokens, LANES), jnp.float32),
            pltpu.VMEM(bias.shape, jnp.float32),
        ],
        compiler_params=pltpu.CompilerParams(vmem_limit_bytes=VMEM_LIMIT),
        name="attention",
    )(valid_len, tokens_in, cotangent, wq, wk, wv, wo, spread, bias)


def pair_kernel(
    pair_ref, bias_ref, wb_ref, tg_ref, tu_ref, td_ref, dpair_ref, sums_ref, totals, grad_top
):
    outer, inner = pl.program_id(0), pl.program_id(1)
    layers, channels, _ = tg_ref.shape
    part_rows, columns, _ = pair_ref.shape
    rows = bias_ref.shape[2]
    tile = part_rows * columns

    @pl.when((outer == 0) & (inner == 0))
    def _():
        totals[...] = jnp.zeros_like(totals)

    @pl.when(inner == 0)
    def _():
        for column in range(columns):
            grad_top[pl.ds(column, rows, stride=columns), :] = dot(
                bias_ref[:, column, :].astype(jnp.bfloat16), wb_ref[...], 0, 0
            )

    field = pair_ref[...].reshape(tile, channels).astype(jnp.float32)
    saved = []
    for layer in range(layers):
        centred = field - jnp.mean(field, axis=-1, keepdims=True)
        variance = jnp.mean(centred * centred, axis=-1, keepdims=True)
        inv_std = lax.rsqrt(variance + EPS_NORM)
        normed = centred * inv_std
        low = normed.astype(jnp.bfloat16)
        gate = dot(low, tg_ref[layer])
        up = dot(low, tu_ref[layer])
        sig = 0.5 * jnp.tanh(0.5 * gate) + 0.5
        act = gate * sig
        hidden = (act * up).astype(jnp.bfloat16)
        saved.append((normed, low, inv_std, gate, up, sig, act, hidden))
        if layer + 1 < layers:
            field = field + dot(hidden, td_ref[layer])
    grad = grad_top[pl.ds(pl.multiple_of(inner * tile, 16), tile), :]
    for layer in reversed(range(layers)):
        normed, low, inv_std, gate, up, sig, act, hidden = saved[layer]
        grad_low = grad.astype(jnp.bfloat16)
        grad_hidden = dot(grad_low, td_ref[layer], 1, 1)
        grad_gate = (grad_hidden * up * (sig + act * (1.0 - sig))).astype(jnp.bfloat16)
        grad_up = (grad_hidden * act).astype(jnp.bfloat16)
        for which, term in enumerate(
            (dot(low, grad_gate, 0, 0), dot(low, grad_up, 0, 0), dot(grad_low, hidden, 0, 0))
        ):
            first = (which * layers + layer) * channels
            totals[first : first + channels] += term
        grad_normed = dot(grad_gate, tg_ref[layer], 1, 1) + dot(grad_up, tu_ref[layer], 1, 1)
        grad = grad + inv_std * (
            grad_normed
            - jnp.mean(grad_normed, axis=-1, keepdims=True)
            - normed * jnp.mean(grad_normed * normed, axis=-1, keepdims=True)
        )
    dpair_ref[...] = grad.astype(jnp.bfloat16).reshape(dpair_ref.shape)

    @pl.when((outer == pl.num_programs(0) - 1) & (inner == pl.num_programs(1) - 1))
    def _():
        sums_ref[...] = totals[...].astype(jnp.bfloat16)


def pair_transitions(pair, bias_grad, w_bias, t_gate, t_up, t_down):
    rows, columns, channels = pair.shape
    heads = bias_grad.shape[0]
    layers, _, hidden = t_gate.shape
    part_rows, part_columns = math.gcd(rows, 64), math.gcd(columns, 16)
    vmem = pl.BlockSpec(memory_space=pltpu.VMEM)
    pair_spec = pl.BlockSpec((part_rows, part_columns, channels), lambda j, i: (i, j, 0))
    sums = (3 * layers * channels, hidden)
    return pl.pallas_call(
        pair_kernel,
        grid=(columns // part_columns, rows // part_rows),
        in_specs=[
            pair_spec,
            pl.BlockSpec((heads, part_columns, rows), lambda j, i: (0, j, 0)),
        ]
        + [vmem] * 4,
        out_specs=[
            pair_spec,
            pl.BlockSpec(sums, lambda j, i: (0, 0)),
        ],
        out_shape=[
            jax.ShapeDtypeStruct(pair.shape, jnp.bfloat16),
            jax.ShapeDtypeStruct(sums, jnp.bfloat16),
        ],
        scratch_shapes=[
            pltpu.VMEM(sums, jnp.float32),
            pltpu.VMEM((rows * part_columns, channels), jnp.float32),
        ],
        compiler_params=pltpu.CompilerParams(vmem_limit_bytes=VMEM_LIMIT),
        name="pair_transitions",
    )(pair, bias_grad, w_bias.T, t_gate, t_up, t_down)


def sum_kernel(
    groups,
    heads,
    divisor,
    part_ref,
    total_ref,
    landed,
    crossed,
    gathered,
    send_a,
    recv_a,
    send_b,
    recv_b,
    send_c,
    recv_c,
):
    samp, head = lax.axis_index("samp"), lax.axis_index("head")
    rows = gathered.shape[1]
    barrier = pltpu.get_barrier_semaphore()
    for k in range(1, groups):
        other = (lax.rem(samp + k, groups), head)
        pl.semaphore_signal(barrier, inc=1, device_id=other, device_id_type=MESH)
    for k in range(1, heads):
        other = (samp, lax.rem(head + k, heads))
        pl.semaphore_signal(barrier, inc=1, device_id=other, device_id_type=MESH)
    pl.semaphore_wait(barrier, groups - 1 + heads - 1)

    def piece(index):
        return pl.ds(pl.multiple_of(index * rows, 16), rows)

    scatter = []
    for k in range(1, groups):
        other = lax.rem(samp + k, groups)
        copy = pltpu.make_async_remote_copy(
            src_ref=part_ref.at[piece(other)],
            dst_ref=landed.at[k],
            send_sem=send_a.at[k],
            recv_sem=recv_a.at[k],
            device_id=(other, head),
            device_id_type=MESH,
        )
        copy.start()
        scatter.append(copy)
    running = part_ref[piece(samp)].astype(jnp.float32)
    for k, copy in enumerate(scatter):
        copy.wait_recv()
        running = running + landed[k + 1].astype(jnp.float32)
    crossed[head] = running.astype(jnp.bfloat16)
    cross = []
    for k in range(1, heads):
        copy = pltpu.make_async_remote_copy(
            src_ref=crossed.at[head],
            dst_ref=crossed.at[head],
            send_sem=send_b.at[k],
            recv_sem=recv_b.at[k],
            device_id=(samp, lax.rem(head + k, heads)),
            device_id_type=MESH,
        )
        copy.start()
        cross.append(copy)
    for copy in cross:
        copy.wait_recv()
    running = crossed[0].astype(jnp.float32)
    for k in range(1, heads):
        running = running + crossed[k].astype(jnp.float32)
    gathered[samp] = running.astype(jnp.bfloat16)
    gather = []
    for k in range(1, groups):
        copy = pltpu.make_async_remote_copy(
            src_ref=gathered.at[samp],
            dst_ref=gathered.at[samp],
            send_sem=send_c.at[k],
            recv_sem=recv_c.at[k],
            device_id=(lax.rem(samp + k, groups), head),
            device_id_type=MESH,
        )
        copy.start()
        gather.append(copy)
    for copy in gather:
        copy.wait_recv()
    for k in range(groups):
        total_ref[k] = gathered[k].astype(jnp.float32) / divisor
    for copy in scatter + cross + gather:
        copy.wait_send()


def sum_everywhere(part, groups, heads, divisor):
    size, width = part.shape
    rows = size // groups
    vmem = pl.BlockSpec(memory_space=pltpu.VMEM)
    return pl.pallas_call(
        functools.partial(sum_kernel, groups, heads, divisor),
        in_specs=[vmem],
        out_specs=vmem,
        out_shape=jax.ShapeDtypeStruct((groups, rows, width), jnp.float32),
        scratch_shapes=[
            pltpu.VMEM((groups, rows, width), jnp.bfloat16),
            pltpu.VMEM((heads, rows, width), jnp.bfloat16),
            pltpu.VMEM((groups, rows, width), jnp.bfloat16),
        ]
        + [pltpu.SemaphoreType.DMA((n,)) for n in (groups, groups, heads, heads, groups, groups)],
        compiler_params=pltpu.CompilerParams(
            collective_id=0, has_side_effects=True, vmem_limit_bytes=VMEM_LIMIT
        ),
        name="sum_everywhere",
    )(part).reshape(size, width)


def exchange_kernel(
    groups,
    head_groups,
    part_ref,
    owned_ref,
    from_pair,
    paired,
    from_chip,
    reduced,
    by_head,
    send_a,
    recv_a,
    send_b,
    recv_b,
    send_c,
    recv_c,
):
    samp, head = lax.axis_index("samp"), lax.axis_index("head")
    heads, columns, _ = from_pair.shape[1:]
    rows = by_head.shape[3]
    chips = groups // 2
    chip, core = samp // 2, lax.rem(samp, 2)
    partner = chip * 2 + 1 - core
    barrier = pltpu.get_barrier_semaphore()
    pl.semaphore_signal(barrier, inc=1, device_id=(partner, head), device_id_type=MESH)
    for k in range(1, chips):
        other = lax.rem(chip + k, chips) * 2 + core
        pl.semaphore_signal(barrier, inc=1, device_id=(other, head), device_id_type=MESH)
    for k in range(1, head_groups):
        other = lax.rem(head + k, head_groups)
        pl.semaphore_signal(barrier, inc=1, device_id=(samp, other), device_id_type=MESH)
    pl.semaphore_wait(barrier, 1 + chips - 1 + head_groups - 1)

    def piece(owner):
        return pl.ds(pl.multiple_of(owner * columns, 16), columns)

    order = list(range(1, chips)) + [0]
    pair_copies = []
    for k in order:
        target = lax.rem(chip + k, chips)
        copy = pltpu.make_async_remote_copy(
            src_ref=part_ref.at[:, piece(target * 2 + 1 - core)],
            dst_ref=from_pair.at[k],
            send_sem=send_a.at[k],
            recv_sem=recv_a.at[k],
            device_id=(partner, head),
            device_id_type=MESH,
        )
        copy.start()
        pair_copies.append(copy)
    chip_copies = []
    running = None
    for k, pair_copy in zip(order, pair_copies):
        target = lax.rem(chip + k, chips)
        pair_copy.wait_recv()
        both = part_ref[:, piece(target * 2 + core)].astype(jnp.float32) + from_pair[k].astype(
            jnp.float32
        )
        if k == 0:
            running = both
            continue
        paired[k] = both.astype(jnp.bfloat16)
        copy = pltpu.make_async_remote_copy(
            src_ref=paired.at[k],
            dst_ref=from_chip.at[k],
            send_sem=send_b.at[k],
            recv_sem=recv_b.at[k],
            device_id=(target * 2 + core, head),
            device_id_type=MESH,
        )
        copy.start()
        chip_copies.append(copy)
    for k, copy in enumerate(chip_copies):
        copy.wait_recv()
        running = running + from_chip[k + 1].astype(jnp.float32)
    low = running.astype(jnp.bfloat16)
    for k in range(head_groups):
        reduced[k] = low[:, :, k * rows : (k + 1) * rows]
    by_head[head] = reduced[head]
    head_copies = []
    for k in range(1, head_groups):
        other = lax.rem(head + k, head_groups)
        copy = pltpu.make_async_remote_copy(
            src_ref=reduced.at[other],
            dst_ref=by_head.at[head],
            send_sem=send_c.at[k],
            recv_sem=recv_c.at[k],
            device_id=(samp, other),
            device_id_type=MESH,
        )
        copy.start()
        head_copies.append(copy)
    for copy in head_copies:
        copy.wait_recv()
    for k in range(head_groups):
        owned_ref[k * heads : (k + 1) * heads] = by_head[k].astype(jnp.float32)
    for copy in pair_copies + chip_copies + head_copies:
        copy.wait_send()


def exchange_bias(parts, groups, head_groups):
    heads, tokens, _ = parts.shape
    columns, rows = tokens // groups, tokens // head_groups
    if groups % 2 or rows % LANES or columns % 16:
        summed = lax.psum_scatter(parts, "samp", scatter_dimension=1, tiled=True)
        owned = lax.all_to_all(summed, "head", split_axis=2, concat_axis=0, tiled=True)
        return owned.astype(jnp.float32)
    chips = groups // 2
    vmem = pl.BlockSpec(memory_space=pltpu.VMEM)
    landing = pltpu.VMEM((chips, heads, columns, tokens), jnp.bfloat16)
    crossing = pltpu.VMEM((head_groups, heads, columns, rows), jnp.bfloat16)
    counts = (chips, chips, chips, chips, head_groups, head_groups)
    return pl.pallas_call(
        functools.partial(exchange_kernel, groups, head_groups),
        in_specs=[vmem],
        out_specs=vmem,
        out_shape=jax.ShapeDtypeStruct((head_groups * heads, columns, rows), jnp.float32),
        scratch_shapes=[landing, landing, landing, crossing, crossing]
        + [pltpu.SemaphoreType.DMA((n,)) for n in counts],
        compiler_params=pltpu.CompilerParams(
            collective_id=1, has_side_effects=True, vmem_limit_bytes=VMEM_LIMIT
        ),
        name="exchange_bias",
    )(parts)


def per_device(
    groups,
    head_groups,
    input_tokens,
    output_cotangent,
    query_weight,
    key_weight,
    value_weight,
    output_weight,
    pair_bias,
    valid_len,
    pair_in,
    w_bias,
    t_gate,
    t_up,
    t_down,
):
    tokens = input_tokens.shape[1]
    token_terms, bias_parts = attention(
        input_tokens,
        output_cotangent,
        query_weight,
        key_weight,
        value_weight,
        output_weight,
        pair_bias,
        valid_len,
    )
    d_tokens = lax.psum_scatter(token_terms, "head", scatter_dimension=1, tiled=True)
    d_tokens = d_tokens.transpose(0, 2, 1)
    owned_grad = exchange_bias(bias_parts, groups, head_groups)
    d_pair, sums = pair_transitions(pair_in, owned_grad, w_bias, t_gate, t_up, t_down)
    totals = sum_everywhere(sums, groups, head_groups, tokens)
    layers, _, hidden = t_gate.shape
    totals = totals.reshape(3, layers, pair_in.shape[2], hidden)
    return (
        d_tokens,
        d_pair,
        totals[0],
        totals[1],
        totals[2].transpose(0, 2, 1),
    )


def solution(mesh):
    placed = (
        P("samp", None, None),
        P("samp", None, None),
        P(None, "head"),
        P(None, "head"),
        P(None, "head"),
        P("head", None),
        P("head", None, None),
        P(),
        P("head", "samp", None),
        P(),
        P(),
        P(),
        P(),
    )
    return jax.shard_map(
        functools.partial(per_device, mesh.shape["samp"], mesh.shape["head"]),
        mesh=mesh,
        in_specs=placed,
        out_specs=(P("samp", None, "head"), P("head", "samp", None), P(), P(), P()),
        check_vma=False,
    )
```

```python
import functools
import math

import jax
import jax.numpy as jnp
from jax import lax
from jax.experimental import pallas as pl
from jax.experimental.pallas import tpu as pltpu
from jax.sharding import PartitionSpec as P

HD = 48
LANES = 128

EPS_NORM = 1e-05
MASKED = -1e30
VMEM_LIMIT = 56 * 1024 * 1024
MESH = pl.DeviceIdType.MESH


def dot(lhs, rhs, lhs_dim=1, rhs_dim=0):
    return lax.dot_general(
        lhs, rhs, (((lhs_dim,), (rhs_dim,)), ((), ())), preferred_element_type=jnp.float32
    )


def attention_kernel(
    rows,
    valid_ref,
    tokens_ref,
    cotangent_ref,
    wq_ref,
    wk_ref,
    wv_ref,
    wo_ref,
    spread_ref,
    bias_ref,
    terms_ref,
    part_ref,
    wide_in,
    wide_out,
    projected,
    attn_grad,
    joined,
    key_sum,
    value_sum,
    bias_sum,
):
    step = pl.program_id(0)
    heads, tokens, _ = bias_ref.shape
    width = heads * LANES
    scale = 1.0 / math.sqrt(HD)

    @pl.when(step == 0)
    def _():
        spread = spread_ref[...]
        for which, ref in enumerate((wq_ref, wk_ref, wv_ref)):
            wide_in[:, which * width : (which + 1) * width] = dot(ref[...], spread, 0, 0).astype(
                jnp.bfloat16
            )
        wide_out[...] = dot(spread, wo_ref[...], 0, 0).astype(jnp.bfloat16)
        bias_sum[...] = jnp.zeros_like(bias_sum)

    projected[...] = dot(tokens_ref[0], wide_in[...]).astype(jnp.bfloat16)
    attn_grad[...] = dot(cotangent_ref[0], wide_out[...], 1, 1).astype(jnp.bfloat16)
    kept = lax.broadcasted_iota(jnp.int32, (1, tokens), 1) < valid_ref[0]

    for head in range(heads):
        q_cols = slice(head * LANES, (head + 1) * LANES)
        k_cols = slice(width + head * LANES, width + (head + 1) * LANES)
        v_cols = slice(2 * width + head * LANES, 2 * width + (head + 1) * LANES)
        keys = projected[:, k_cols]
        values = projected[:, v_cols]
        for block in range(tokens // rows):
            span = slice(block * rows, (block + 1) * rows)
            query = projected[span, q_cols]
            grad_out = attn_grad[span, q_cols]
            scores = dot(query, keys, 1, 1) * scale + bias_ref[head, span].astype(jnp.float32)
            scores = jnp.where(kept, scores, MASKED)
            exp_scores = jnp.exp(scores - jnp.max(scores, axis=-1, keepdims=True))
            probs = exp_scores * (1.0 / jnp.sum(exp_scores, axis=-1, keepdims=True))
            grad_probs = dot(grad_out, values, 1, 1)
            delta = jnp.sum(probs * grad_probs, axis=-1, keepdims=True)
            grad_scores = probs * (grad_probs - delta)
            scores_low = grad_scores.astype(jnp.bfloat16)
            bias_sum[head, span] += grad_scores
            joined[span, q_cols] = (dot(scores_low, keys) * scale).astype(jnp.bfloat16)
            key_term = dot(scores_low, query, 0, 0)
            value_term = dot(probs.astype(jnp.bfloat16), grad_out, 0, 0)
            if block == 0:
                key_sum[...] = key_term
                value_sum[...] = value_term
            else:
                key_sum[...] += key_term
                value_sum[...] += value_term
        joined[:, k_cols] = (key_sum[...] * scale).astype(jnp.bfloat16)
        joined[:, v_cols] = value_sum[...].astype(jnp.bfloat16)

    terms_ref[0] = dot(wide_in[...], joined[...], 1, 1).astype(jnp.bfloat16)

    @pl.when(step == pl.num_programs(0) - 1)
    def _():
        for head in range(heads):
            part_ref[head] = bias_sum[head].T.astype(jnp.bfloat16)


def attention(tokens_in, cotangent, wq, wk, wv, wo, bias, valid_len):
    samples, tokens, features = tokens_in.shape
    heads = bias.shape[0]
    width = heads * LANES
    source = lax.broadcasted_iota(jnp.int32, (heads * HD, width), 0)
    place = lax.broadcasted_iota(jnp.int32, (heads * HD, width), 1)
    spread = (place == (source // HD) * LANES + source % HD).astype(jnp.bfloat16)
    vmem = pl.BlockSpec(memory_space=pltpu.VMEM)
    per_sample = pl.BlockSpec((1, tokens, features), lambda s: (s, 0, 0))
    whole_bias = pl.BlockSpec(bias.shape, lambda s: (0, 0, 0))
    return pl.pallas_call(
        functools.partial(attention_kernel, min(128, tokens)),
        grid=(samples,),
        in_specs=[pl.BlockSpec(memory_space=pltpu.SMEM), per_sample, per_sample]
        + [vmem] * 6,
        out_specs=[pl.BlockSpec((1, features, tokens), lambda s: (s, 0, 0)), whole_bias],
        out_shape=[
            jax.ShapeDtypeStruct((samples, features, tokens), jnp.bfloat16),
            jax.ShapeDtypeStruct(bias.shape, jnp.bfloat16),
        ],
        scratch_shapes=[
            pltpu.VMEM((features, 3 * width), jnp.bfloat16),
            pltpu.VMEM((width, features), jnp.bfloat16),
            pltpu.VMEM((tokens, 3 * width), jnp.bfloat16),
            pltpu.VMEM((tokens, width), jnp.bfloat16),
            pltpu.VMEM((tokens, 3 * width), jnp.bfloat16),
            pltpu.VMEM((tokens, LANES), jnp.float32),
            pltpu.VMEM((tokens, LANES), jnp.float32),
            pltpu.VMEM(bias.shape, jnp.float32),
        ],
        compiler_params=pltpu.CompilerParams(vmem_limit_bytes=VMEM_LIMIT),
        name="attention",
    )(valid_len, tokens_in, cotangent, wq.T, wk.T, wv.T, wo, spread, bias)


def pair_kernel(
    pair_ref, bias_ref, wb_ref, tg_ref, tu_ref, td_ref, dpair_ref, sums_ref, totals, grad_top
):
    outer, inner = pl.program_id(0), pl.program_id(1)
    layers, channels, _ = tg_ref.shape
    part_rows, columns, _ = pair_ref.shape
    rows = bias_ref.shape[2]
    tile = part_rows * columns

    @pl.when((outer == 0) & (inner == 0))
    def _():
        totals[...] = jnp.zeros_like(totals)

    @pl.when(inner == 0)
    def _():
        for column in range(columns):
            grad_top[pl.ds(column, rows, stride=columns), :] = dot(
                bias_ref[:, column, :].astype(jnp.bfloat16), wb_ref[...], 0, 0
            )

    field = pair_ref[...].reshape(tile, channels).astype(jnp.float32)
    saved = []
    for layer in range(layers):
        centred = field - jnp.mean(field, axis=-1, keepdims=True)
        variance = jnp.mean(centred * centred, axis=-1, keepdims=True)
        inv_std = lax.rsqrt(variance + EPS_NORM)
        normed = centred * inv_std
        low = normed.astype(jnp.bfloat16)
        gate = dot(low, tg_ref[layer]).astype(jnp.bfloat16)
        up = dot(low, tu_ref[layer]).astype(jnp.bfloat16)
        sig = 0.5 * jnp.tanh(0.5 * gate) + 0.5
        act = gate * sig
        hidden = act * up
        saved.append((normed, low, inv_std, gate, up, sig, act, hidden))
        if layer + 1 < layers:
            field = field + dot(hidden, td_ref[layer])
    grad = grad_top[pl.ds(pl.multiple_of(inner * tile, 16), tile), :]
    for layer in reversed(range(layers)):
        normed, low, inv_std, gate, up, sig, act, hidden = saved[layer]
        grad_low = grad.astype(jnp.bfloat16)
        grad_hidden = dot(grad_low, td_ref[layer], 1, 1).astype(jnp.bfloat16)
        grad_gate = grad_hidden * up * (sig + act * (1.0 - sig))
        grad_up = grad_hidden * act
        for which, term in enumerate(
            (dot(low, grad_gate, 0, 0), dot(low, grad_up, 0, 0), dot(grad_low, hidden, 0, 0))
        ):
            first = (which * layers + layer) * channels
            totals[first : first + channels] += term
        grad_normed = dot(grad_gate, tg_ref[layer], 1, 1) + dot(grad_up, tu_ref[layer], 1, 1)
        grad = grad + inv_std * (
            grad_normed
            - jnp.mean(grad_normed, axis=-1, keepdims=True)
            - normed * jnp.mean(grad_normed * normed, axis=-1, keepdims=True)
        )
    dpair_ref[...] = grad.astype(jnp.bfloat16).reshape(dpair_ref.shape)

    @pl.when((outer == pl.num_programs(0) - 1) & (inner == pl.num_programs(1) - 1))
    def _():
        sums_ref[...] = totals[...].astype(jnp.bfloat16)


def pair_transitions(pair, bias_grad, w_bias, t_gate, t_up, t_down):
    rows, columns, channels = pair.shape
    heads = bias_grad.shape[0]
    layers, _, hidden = t_gate.shape
    part_rows, part_columns = math.gcd(rows, 64), math.gcd(columns, 16)
    vmem = pl.BlockSpec(memory_space=pltpu.VMEM)
    pair_spec = pl.BlockSpec((part_rows, part_columns, channels), lambda j, i: (i, j, 0))
    sums = (3 * layers * channels, hidden)
    return pl.pallas_call(
        pair_kernel,
        grid=(columns // part_columns, rows // part_rows),
        in_specs=[
            pair_spec,
            pl.BlockSpec((heads, part_columns, rows), lambda j, i: (0, j, 0)),
        ]
        + [vmem] * 4,
        out_specs=[
            pair_spec,
            pl.BlockSpec(sums, lambda j, i: (0, 0)),
        ],
        out_shape=[
            jax.ShapeDtypeStruct(pair.shape, jnp.bfloat16),
            jax.ShapeDtypeStruct(sums, jnp.bfloat16),
        ],
        scratch_shapes=[
            pltpu.VMEM(sums, jnp.float32),
            pltpu.VMEM((rows * part_columns, channels), jnp.float32),
        ],
        compiler_params=pltpu.CompilerParams(vmem_limit_bytes=VMEM_LIMIT),
        name="pair_transitions",
    )(pair, bias_grad, w_bias.T, t_gate, t_up, t_down)


def sum_kernel(
    groups,
    heads,
    divisor,
    part_ref,
    total_ref,
    landed,
    crossed,
    gathered,
    send_a,
    recv_a,
    send_b,
    recv_b,
    send_c,
    recv_c,
):
    samp, head = lax.axis_index("samp"), lax.axis_index("head")
    rows = gathered.shape[1]
    barrier = pltpu.get_barrier_semaphore()
    for k in range(1, groups):
        other = (lax.rem(samp + k, groups), head)
        pl.semaphore_signal(barrier, inc=1, device_id=other, device_id_type=MESH)
    for k in range(1, heads):
        other = (samp, lax.rem(head + k, heads))
        pl.semaphore_signal(barrier, inc=1, device_id=other, device_id_type=MESH)
    pl.semaphore_wait(barrier, groups - 1 + heads - 1)

    def piece(index):
        return pl.ds(pl.multiple_of(index * rows, 16), rows)

    scatter = []
    for k in range(1, groups):
        other = lax.rem(samp + k, groups)
        copy = pltpu.make_async_remote_copy(
            src_ref=part_ref.at[piece(other)],
            dst_ref=landed.at[k],
            send_sem=send_a.at[k],
            recv_sem=recv_a.at[k],
            device_id=(other, head),
            device_id_type=MESH,
        )
        copy.start()
        scatter.append(copy)
    running = part_ref[piece(samp)].astype(jnp.float32)
    for k, copy in enumerate(scatter):
        copy.wait_recv()
        running = running + landed[k + 1].astype(jnp.float32)
    crossed[head] = running.astype(jnp.bfloat16)
    cross = []
    for k in range(1, heads):
        copy = pltpu.make_async_remote_copy(
            src_ref=crossed.at[head],
            dst_ref=crossed.at[head],
            send_sem=send_b.at[k],
            recv_sem=recv_b.at[k],
            device_id=(samp, lax.rem(head + k, heads)),
            device_id_type=MESH,
        )
        copy.start()
        cross.append(copy)
    for copy in cross:
        copy.wait_recv()
    running = crossed[0].astype(jnp.float32)
    for k in range(1, heads):
        running = running + crossed[k].astype(jnp.float32)
    gathered[samp] = running.astype(jnp.bfloat16)
    gather = []
    for k in range(1, groups):
        copy = pltpu.make_async_remote_copy(
            src_ref=gathered.at[samp],
            dst_ref=gathered.at[samp],
            send_sem=send_c.at[k],
            recv_sem=recv_c.at[k],
            device_id=(lax.rem(samp + k, groups), head),
            device_id_type=MESH,
        )
        copy.start()
        gather.append(copy)
    for copy in gather:
        copy.wait_recv()
    for k in range(groups):
        total_ref[k] = gathered[k].astype(jnp.float32) / divisor
    for copy in scatter + cross + gather:
        copy.wait_send()


def sum_everywhere(part, groups, heads, divisor):
    size, width = part.shape
    rows = size // groups
    vmem = pl.BlockSpec(memory_space=pltpu.VMEM)
    return pl.pallas_call(
        functools.partial(sum_kernel, groups, heads, divisor),
        in_specs=[vmem],
        out_specs=vmem,
        out_shape=jax.ShapeDtypeStruct((groups, rows, width), jnp.float32),
        scratch_shapes=[
            pltpu.VMEM((groups, rows, width), jnp.bfloat16),
            pltpu.VMEM((heads, rows, width), jnp.bfloat16),
            pltpu.VMEM((groups, rows, width), jnp.bfloat16),
        ]
        + [pltpu.SemaphoreType.DMA((n,)) for n in (groups, groups, heads, heads, groups, groups)],
        compiler_params=pltpu.CompilerParams(
            collective_id=0, has_side_effects=True, vmem_limit_bytes=VMEM_LIMIT
        ),
        name="sum_everywhere",
    )(part).reshape(size, width)


def exchange_kernel(
    groups,
    head_groups,
    part_ref,
    owned_ref,
    from_pair,
    paired,
    from_chip,
    reduced,
    by_head,
    send_a,
    recv_a,
    send_b,
    recv_b,
    send_c,
    recv_c,
):
    samp, head = lax.axis_index("samp"), lax.axis_index("head")
    heads, columns, _ = from_pair.shape[1:]
    rows = by_head.shape[3]
    chips = groups // 2
    chip, core = samp // 2, lax.rem(samp, 2)
    partner = chip * 2 + 1 - core
    barrier = pltpu.get_barrier_semaphore()
    pl.semaphore_signal(barrier, inc=1, device_id=(partner, head), device_id_type=MESH)
    for k in range(1, chips):
        other = lax.rem(chip + k, chips) * 2 + core
        pl.semaphore_signal(barrier, inc=1, device_id=(other, head), device_id_type=MESH)
    for k in range(1, head_groups):
        other = lax.rem(head + k, head_groups)
        pl.semaphore_signal(barrier, inc=1, device_id=(samp, other), device_id_type=MESH)
    pl.semaphore_wait(barrier, 1 + chips - 1 + head_groups - 1)

    def piece(owner):
        return pl.ds(pl.multiple_of(owner * columns, 16), columns)

    order = list(range(1, chips)) + [0]
    pair_copies = []
    for k in order:
        target = lax.rem(chip + k, chips)
        copy = pltpu.make_async_remote_copy(
            src_ref=part_ref.at[:, piece(target * 2 + 1 - core)],
            dst_ref=from_pair.at[k],
            send_sem=send_a.at[k],
            recv_sem=recv_a.at[k],
            device_id=(partner, head),
            device_id_type=MESH,
        )
        copy.start()
        pair_copies.append(copy)
    chip_copies = []
    running = None
    for k, pair_copy in zip(order, pair_copies):
        target = lax.rem(chip + k, chips)
        pair_copy.wait_recv()
        both = part_ref[:, piece(target * 2 + core)].astype(jnp.float32) + from_pair[k].astype(
            jnp.float32
        )
        if k == 0:
            running = both
            continue
        paired[k] = both.astype(jnp.bfloat16)
        copy = pltpu.make_async_remote_copy(
            src_ref=paired.at[k],
            dst_ref=from_chip.at[k],
            send_sem=send_b.at[k],
            recv_sem=recv_b.at[k],
            device_id=(target * 2 + core, head),
            device_id_type=MESH,
        )
        copy.start()
        chip_copies.append(copy)
    for k, copy in enumerate(chip_copies):
        copy.wait_recv()
        running = running + from_chip[k + 1].astype(jnp.float32)
    low = running.astype(jnp.bfloat16)
    for k in range(head_groups):
        reduced[k] = low[:, :, k * rows : (k + 1) * rows]
    by_head[head] = reduced[head]
    head_copies = []
    for k in range(1, head_groups):
        other = lax.rem(head + k, head_groups)
        copy = pltpu.make_async_remote_copy(
            src_ref=reduced.at[other],
            dst_ref=by_head.at[head],
            send_sem=send_c.at[k],
            recv_sem=recv_c.at[k],
            device_id=(samp, other),
            device_id_type=MESH,
        )
        copy.start()
        head_copies.append(copy)
    for copy in head_copies:
        copy.wait_recv()
    for k in range(head_groups):
        owned_ref[k * heads : (k + 1) * heads] = by_head[k].astype(jnp.float32)
    for copy in pair_copies + chip_copies + head_copies:
        copy.wait_send()


def exchange_bias(parts, groups, head_groups):
    heads, tokens, _ = parts.shape
    columns, rows = tokens // groups, tokens // head_groups
    if groups % 2 or rows % LANES or columns % 16:
        summed = lax.psum_scatter(parts, "samp", scatter_dimension=1, tiled=True)
        owned = lax.all_to_all(summed, "head", split_axis=2, concat_axis=0, tiled=True)
        return owned.astype(jnp.float32)
    chips = groups // 2
    vmem = pl.BlockSpec(memory_space=pltpu.VMEM)
    landing = pltpu.VMEM((chips, heads, columns, tokens), jnp.bfloat16)
    crossing = pltpu.VMEM((head_groups, heads, columns, rows), jnp.bfloat16)
    counts = (chips, chips, chips, chips, head_groups, head_groups)
    return pl.pallas_call(
        functools.partial(exchange_kernel, groups, head_groups),
        in_specs=[vmem],
        out_specs=vmem,
        out_shape=jax.ShapeDtypeStruct((head_groups * heads, columns, rows), jnp.float32),
        scratch_shapes=[landing, landing, landing, crossing, crossing]
        + [pltpu.SemaphoreType.DMA((n,)) for n in counts],
        compiler_params=pltpu.CompilerParams(
            collective_id=1, has_side_effects=True, vmem_limit_bytes=VMEM_LIMIT
        ),
        name="exchange_bias",
    )(parts)


def per_device(
    groups,
    head_groups,
    input_tokens,
    output_cotangent,
    query_weight,
    key_weight,
    value_weight,
    output_weight,
    pair_bias,
    valid_len,
    pair_in,
    w_bias,
    t_gate,
    t_up,
    t_down,
):
    tokens = input_tokens.shape[1]
    token_terms, bias_parts = attention(
        input_tokens,
        output_cotangent,
        query_weight,
        key_weight,
        value_weight,
        output_weight,
        pair_bias,
        valid_len,
    )
    d_tokens = lax.psum_scatter(token_terms, "head", scatter_dimension=1, tiled=True)
    d_tokens = d_tokens.transpose(0, 2, 1)
    owned_grad = exchange_bias(bias_parts, groups, head_groups)
    d_pair, sums = pair_transitions(pair_in, owned_grad, w_bias, t_gate, t_up, t_down)
    totals = sum_everywhere(sums, groups, head_groups, tokens)
    layers, _, hidden = t_gate.shape
    totals = totals.reshape(3, layers, pair_in.shape[2], hidden)
    return (
        d_tokens,
        d_pair,
        totals[0],
        totals[1],
        totals[2].transpose(0, 2, 1),
    )


def solution(mesh):
    placed = (
        P("samp", None, None),
        P("samp", None, None),
        P(None, "head"),
        P(None, "head"),
        P(None, "head"),
        P("head", None),
        P("head", None, None),
        P(),
        P("head", "samp", None),
        P(),
        P(),
        P(),
        P(),
    )
    return jax.shard_map(
        functools.partial(per_device, mesh.shape["samp"], mesh.shape["head"]),
        mesh=mesh,
        in_specs=placed,
        out_specs=(P("samp", None, "head"), P("head", "samp", None), P(), P(), P()),
        check_vma=False,
    )
```

```python
import functools
import math

import jax
import jax.numpy as jnp
from jax import lax
from jax.experimental import pallas as pl
from jax.experimental.pallas import tpu as pltpu
from jax.sharding import PartitionSpec as P

HD = 48
LANES = 128

EPS_NORM = 1e-05
MASKED = -1e30
VMEM_LIMIT = 56 * 1024 * 1024
MESH = pl.DeviceIdType.MESH


def dot(lhs, rhs, lhs_dim=1, rhs_dim=0):
    return lax.dot_general(
        lhs, rhs, (((lhs_dim,), (rhs_dim,)), ((), ())), preferred_element_type=jnp.float32
    )


def attention_kernel(
    rows,
    valid_ref,
    tokens_ref,
    cotangent_ref,
    wq_ref,
    wk_ref,
    wv_ref,
    wo_ref,
    spread_ref,
    bias_ref,
    terms_ref,
    part_ref,
    wide_in,
    wide_out,
    projected,
    attn_grad,
    joined,
    key_sum,
    value_sum,
    bias_sum,
):
    step = pl.program_id(0)
    heads, tokens, _ = bias_ref.shape
    width = heads * LANES
    scale = 1.0 / math.sqrt(HD)

    @pl.when(step == 0)
    def _():
        spread = spread_ref[...]
        for which, ref in enumerate((wq_ref, wk_ref, wv_ref)):
            wide_in[:, which * width : (which + 1) * width] = dot(ref[...], spread, 0, 0).astype(
                jnp.bfloat16
            )
        wide_out[...] = dot(spread, wo_ref[...], 0, 0).astype(jnp.bfloat16)
        bias_sum[...] = jnp.zeros_like(bias_sum)

    projected[...] = dot(tokens_ref[0], wide_in[...]).astype(jnp.bfloat16)
    attn_grad[...] = dot(cotangent_ref[0], wide_out[...], 1, 1).astype(jnp.bfloat16)
    kept = lax.broadcasted_iota(jnp.int32, (1, tokens), 1) < valid_ref[0]

    for head in range(heads):
        q_cols = slice(head * LANES, (head + 1) * LANES)
        k_cols = slice(width + head * LANES, width + (head + 1) * LANES)
        v_cols = slice(2 * width + head * LANES, 2 * width + (head + 1) * LANES)
        keys = projected[:, k_cols]
        values = projected[:, v_cols]
        for block in range(tokens // rows):
            span = slice(block * rows, (block + 1) * rows)
            query = projected[span, q_cols]
            grad_out = attn_grad[span, q_cols]
            scores = dot(query, keys, 1, 1) * scale + bias_ref[head, span].astype(jnp.float32)
            scores = jnp.where(kept, scores, MASKED)
            exp_scores = jnp.exp(scores - jnp.max(scores, axis=-1, keepdims=True))
            probs = exp_scores * (1.0 / jnp.sum(exp_scores, axis=-1, keepdims=True))
            grad_probs = dot(grad_out, values, 1, 1)
            delta = jnp.sum(probs * grad_probs, axis=-1, keepdims=True)
            grad_scores = probs * (grad_probs - delta)
            scores_low = grad_scores.astype(jnp.bfloat16)
            bias_sum[head, span] += grad_scores
            joined[span, q_cols] = (dot(scores_low, keys) * scale).astype(jnp.bfloat16)
            key_term = dot(scores_low, query, 0, 0)
            value_term = dot(probs.astype(jnp.bfloat16), grad_out, 0, 0)
            if block == 0:
                key_sum[...] = key_term
                value_sum[...] = value_term
            else:
                key_sum[...] += key_term
                value_sum[...] += value_term
        joined[:, k_cols] = (key_sum[...] * scale).astype(jnp.bfloat16)
        joined[:, v_cols] = value_sum[...].astype(jnp.bfloat16)

    terms_ref[0] = dot(wide_in[...], joined[...], 1, 1).astype(jnp.bfloat16)

    @pl.when(step == pl.num_programs(0) - 1)
    def _():
        for head in range(heads):
            part_ref[head] = bias_sum[head].T.astype(jnp.bfloat16)


def attention(tokens_in, cotangent, wq, wk, wv, wo, bias, valid_len):
    samples, tokens, features = tokens_in.shape
    heads = bias.shape[0]
    width = heads * LANES
    source = lax.broadcasted_iota(jnp.int32, (heads * HD, width), 0)
    place = lax.broadcasted_iota(jnp.int32, (heads * HD, width), 1)
    spread = (place == (source // HD) * LANES + source % HD).astype(jnp.bfloat16)
    vmem = pl.BlockSpec(memory_space=pltpu.VMEM)
    per_sample = pl.BlockSpec((1, tokens, features), lambda s: (s, 0, 0))
    whole_bias = pl.BlockSpec(bias.shape, lambda s: (0, 0, 0))
    return pl.pallas_call(
        functools.partial(attention_kernel, math.gcd(256, tokens)),
        grid=(samples,),
        in_specs=[pl.BlockSpec(memory_space=pltpu.SMEM), per_sample, per_sample]
        + [vmem] * 6,
        out_specs=[pl.BlockSpec((1, features, tokens), lambda s: (s, 0, 0)), whole_bias],
        out_shape=[
            jax.ShapeDtypeStruct((samples, features, tokens), jnp.bfloat16),
            jax.ShapeDtypeStruct(bias.shape, jnp.bfloat16),
        ],
        scratch_shapes=[
            pltpu.VMEM((features, 3 * width), jnp.bfloat16),
            pltpu.VMEM((width, features), jnp.bfloat16),
            pltpu.VMEM((tokens, 3 * width), jnp.bfloat16),
            pltpu.VMEM((tokens, width), jnp.bfloat16),
            pltpu.VMEM((tokens, 3 * width), jnp.bfloat16),
            pltpu.VMEM((tokens, LANES), jnp.float32),
            pltpu.VMEM((tokens, LANES), jnp.float32),
            pltpu.VMEM(bias.shape, jnp.float32),
        ],
        compiler_params=pltpu.CompilerParams(vmem_limit_bytes=VMEM_LIMIT),
        name="attention",
    )(valid_len, tokens_in, cotangent, wq.T, wk.T, wv.T, wo, spread, bias)


def pair_kernel(
    pair_ref, bias_ref, wb_ref, tg_ref, tu_ref, td_ref, dpair_ref, sums_ref, totals, grad_top
):
    outer, inner = pl.program_id(0), pl.program_id(1)
    layers, channels, _ = tg_ref.shape
    part_rows, columns, _ = pair_ref.shape
    rows = bias_ref.shape[2]
    tile = part_rows * columns

    @pl.when((outer == 0) & (inner == 0))
    def _():
        totals[...] = jnp.zeros_like(totals)

    @pl.when(inner == 0)
    def _():
        for column in range(columns):
            grad_top[pl.ds(column, rows, stride=columns), :] = dot(
                bias_ref[:, column, :].astype(jnp.bfloat16), wb_ref[...], 0, 0
            )

    field = pair_ref[...].reshape(tile, channels).astype(jnp.float32)
    saved = []
    for layer in range(layers):
        centred = field - jnp.mean(field, axis=-1, keepdims=True)
        variance = jnp.mean(centred * centred, axis=-1, keepdims=True)
        inv_std = lax.rsqrt(variance + EPS_NORM)
        normed = centred * inv_std
        low = normed.astype(jnp.bfloat16)
        gate = dot(low, tg_ref[layer]).astype(jnp.bfloat16)
        up = dot(low, tu_ref[layer]).astype(jnp.bfloat16)
        sig = 0.5 * jnp.tanh(0.5 * gate) + 0.5
        act = gate * sig
        hidden = act * up
        saved.append((normed, low, inv_std, gate, up, sig, act, hidden))
        if layer + 1 < layers:
            field = field + dot(hidden, td_ref[layer])
    grad = grad_top[pl.ds(pl.multiple_of(inner * tile, 16), tile), :]
    for layer in reversed(range(layers)):
        normed, low, inv_std, gate, up, sig, act, hidden = saved[layer]
        grad_low = grad.astype(jnp.bfloat16)
        grad_hidden = dot(grad_low, td_ref[layer], 1, 1).astype(jnp.bfloat16)
        grad_gate = grad_hidden * up * (sig + act * (1.0 - sig))
        grad_up = grad_hidden * act
        for which, term in enumerate(
            (dot(low, grad_gate, 0, 0), dot(low, grad_up, 0, 0), dot(grad_low, hidden, 0, 0))
        ):
            first = (which * layers + layer) * channels
            totals[first : first + channels] += term
        grad_normed = dot(grad_gate, tg_ref[layer], 1, 1) + dot(grad_up, tu_ref[layer], 1, 1)
        grad = grad + inv_std * (
            grad_normed
            - jnp.mean(grad_normed, axis=-1, keepdims=True)
            - normed * jnp.mean(grad_normed * normed, axis=-1, keepdims=True)
        )
    dpair_ref[...] = grad.astype(jnp.bfloat16).reshape(dpair_ref.shape)

    @pl.when((outer == pl.num_programs(0) - 1) & (inner == pl.num_programs(1) - 1))
    def _():
        sums_ref[...] = totals[...].astype(jnp.bfloat16)


def pair_transitions(pair, bias_grad, w_bias, t_gate, t_up, t_down):
    rows, columns, channels = pair.shape
    heads = bias_grad.shape[0]
    layers, _, hidden = t_gate.shape
    part_rows, part_columns = math.gcd(rows, 64), math.gcd(columns, 16)
    vmem = pl.BlockSpec(memory_space=pltpu.VMEM)
    pair_spec = pl.BlockSpec((part_rows, part_columns, channels), lambda j, i: (i, j, 0))
    sums = (3 * layers * channels, hidden)
    return pl.pallas_call(
        pair_kernel,
        grid=(columns // part_columns, rows // part_rows),
        in_specs=[
            pair_spec,
            pl.BlockSpec((heads, part_columns, rows), lambda j, i: (0, j, 0)),
        ]
        + [vmem] * 4,
        out_specs=[
            pair_spec,
            pl.BlockSpec(sums, lambda j, i: (0, 0)),
        ],
        out_shape=[
            jax.ShapeDtypeStruct(pair.shape, jnp.bfloat16),
            jax.ShapeDtypeStruct(sums, jnp.bfloat16),
        ],
        scratch_shapes=[
            pltpu.VMEM(sums, jnp.float32),
            pltpu.VMEM((rows * part_columns, channels), jnp.float32),
        ],
        compiler_params=pltpu.CompilerParams(vmem_limit_bytes=VMEM_LIMIT),
        name="pair_transitions",
    )(pair, bias_grad, w_bias.T, t_gate, t_up, t_down)


def sum_kernel(
    groups,
    heads,
    divisor,
    part_ref,
    total_ref,
    landed,
    crossed,
    gathered,
    send_a,
    recv_a,
    send_b,
    recv_b,
    send_c,
    recv_c,
):
    samp, head = lax.axis_index("samp"), lax.axis_index("head")
    rows = gathered.shape[1]
    barrier = pltpu.get_barrier_semaphore()
    for k in range(1, groups):
        other = (lax.rem(samp + k, groups), head)
        pl.semaphore_signal(barrier, inc=1, device_id=other, device_id_type=MESH)
    for k in range(1, heads):
        other = (samp, lax.rem(head + k, heads))
        pl.semaphore_signal(barrier, inc=1, device_id=other, device_id_type=MESH)
    pl.semaphore_wait(barrier, groups - 1 + heads - 1)

    def piece(index):
        return pl.ds(pl.multiple_of(index * rows, 16), rows)

    scatter = []
    for k in range(1, groups):
        other = lax.rem(samp + k, groups)
        copy = pltpu.make_async_remote_copy(
            src_ref=part_ref.at[piece(other)],
            dst_ref=landed.at[k],
            send_sem=send_a.at[k],
            recv_sem=recv_a.at[k],
            device_id=(other, head),
            device_id_type=MESH,
        )
        copy.start()
        scatter.append(copy)
    running = part_ref[piece(samp)].astype(jnp.float32)
    for k, copy in enumerate(scatter):
        copy.wait_recv()
        running = running + landed[k + 1].astype(jnp.float32)
    crossed[head] = running.astype(jnp.bfloat16)
    cross = []
    for k in range(1, heads):
        copy = pltpu.make_async_remote_copy(
            src_ref=crossed.at[head],
            dst_ref=crossed.at[head],
            send_sem=send_b.at[k],
            recv_sem=recv_b.at[k],
            device_id=(samp, lax.rem(head + k, heads)),
            device_id_type=MESH,
        )
        copy.start()
        cross.append(copy)
    for copy in cross:
        copy.wait_recv()
    running = crossed[0].astype(jnp.float32)
    for k in range(1, heads):
        running = running + crossed[k].astype(jnp.float32)
    gathered[samp] = running.astype(jnp.bfloat16)
    gather = []
    for k in range(1, groups):
        copy = pltpu.make_async_remote_copy(
            src_ref=gathered.at[samp],
            dst_ref=gathered.at[samp],
            send_sem=send_c.at[k],
            recv_sem=recv_c.at[k],
            device_id=(lax.rem(samp + k, groups), head),
            device_id_type=MESH,
        )
        copy.start()
        gather.append(copy)
    for copy in gather:
        copy.wait_recv()
    for k in range(groups):
        total_ref[k] = gathered[k].astype(jnp.float32) / divisor
    for copy in scatter + cross + gather:
        copy.wait_send()


def sum_everywhere(part, groups, heads, divisor):
    size, width = part.shape
    rows = size // groups
    vmem = pl.BlockSpec(memory_space=pltpu.VMEM)
    return pl.pallas_call(
        functools.partial(sum_kernel, groups, heads, divisor),
        in_specs=[vmem],
        out_specs=vmem,
        out_shape=jax.ShapeDtypeStruct((groups, rows, width), jnp.float32),
        scratch_shapes=[
            pltpu.VMEM((groups, rows, width), jnp.bfloat16),
            pltpu.VMEM((heads, rows, width), jnp.bfloat16),
            pltpu.VMEM((groups, rows, width), jnp.bfloat16),
        ]
        + [pltpu.SemaphoreType.DMA((n,)) for n in (groups, groups, heads, heads, groups, groups)],
        compiler_params=pltpu.CompilerParams(
            collective_id=0, has_side_effects=True, vmem_limit_bytes=VMEM_LIMIT
        ),
        name="sum_everywhere",
    )(part).reshape(size, width)


def exchange_kernel(
    groups,
    head_groups,
    part_ref,
    owned_ref,
    from_pair,
    paired,
    from_chip,
    reduced,
    by_head,
    send_a,
    recv_a,
    send_b,
    recv_b,
    send_c,
    recv_c,
):
    samp, head = lax.axis_index("samp"), lax.axis_index("head")
    heads, columns, _ = from_pair.shape[1:]
    rows = by_head.shape[3]
    chips = groups // 2
    chip, core = samp // 2, lax.rem(samp, 2)
    partner = chip * 2 + 1 - core
    barrier = pltpu.get_barrier_semaphore()
    pl.semaphore_signal(barrier, inc=1, device_id=(partner, head), device_id_type=MESH)
    for k in range(1, chips):
        other = lax.rem(chip + k, chips) * 2 + core
        pl.semaphore_signal(barrier, inc=1, device_id=(other, head), device_id_type=MESH)
    for k in range(1, head_groups):
        other = lax.rem(head + k, head_groups)
        pl.semaphore_signal(barrier, inc=1, device_id=(samp, other), device_id_type=MESH)
    pl.semaphore_wait(barrier, 1 + chips - 1 + head_groups - 1)

    def piece(owner):
        return pl.ds(pl.multiple_of(owner * columns, 16), columns)

    order = list(range(1, chips)) + [0]
    pair_copies = []
    for k in order:
        target = lax.rem(chip + k, chips)
        copy = pltpu.make_async_remote_copy(
            src_ref=part_ref.at[:, piece(target * 2 + 1 - core)],
            dst_ref=from_pair.at[k],
            send_sem=send_a.at[k],
            recv_sem=recv_a.at[k],
            device_id=(partner, head),
            device_id_type=MESH,
        )
        copy.start()
        pair_copies.append(copy)
    chip_copies = []
    running = None
    for k, pair_copy in zip(order, pair_copies):
        target = lax.rem(chip + k, chips)
        pair_copy.wait_recv()
        both = part_ref[:, piece(target * 2 + core)].astype(jnp.float32) + from_pair[k].astype(
            jnp.float32
        )
        if k == 0:
            running = both
            continue
        paired[k] = both.astype(jnp.bfloat16)
        copy = pltpu.make_async_remote_copy(
            src_ref=paired.at[k],
            dst_ref=from_chip.at[k],
            send_sem=send_b.at[k],
            recv_sem=recv_b.at[k],
            device_id=(target * 2 + core, head),
            device_id_type=MESH,
        )
        copy.start()
        chip_copies.append(copy)
    for k, copy in enumerate(chip_copies):
        copy.wait_recv()
        running = running + from_chip[k + 1].astype(jnp.float32)
    low = running.astype(jnp.bfloat16)
    for k in range(head_groups):
        reduced[k] = low[:, :, k * rows : (k + 1) * rows]
    by_head[head] = reduced[head]
    head_copies = []
    for k in range(1, head_groups):
        other = lax.rem(head + k, head_groups)
        copy = pltpu.make_async_remote_copy(
            src_ref=reduced.at[other],
            dst_ref=by_head.at[head],
            send_sem=send_c.at[k],
            recv_sem=recv_c.at[k],
            device_id=(samp, other),
            device_id_type=MESH,
        )
        copy.start()
        head_copies.append(copy)
    for copy in head_copies:
        copy.wait_recv()
    for k in range(head_groups):
        owned_ref[k * heads : (k + 1) * heads] = by_head[k].astype(jnp.float32)
    for copy in pair_copies + chip_copies + head_copies:
        copy.wait_send()


def exchange_bias(parts, groups, head_groups):
    heads, tokens, _ = parts.shape
    columns, rows = tokens // groups, tokens // head_groups
    if groups % 2 or rows % LANES or columns % 16:
        summed = lax.psum_scatter(parts, "samp", scatter_dimension=1, tiled=True)
        owned = lax.all_to_all(summed, "head", split_axis=2, concat_axis=0, tiled=True)
        return owned.astype(jnp.float32)
    chips = groups // 2
    vmem = pl.BlockSpec(memory_space=pltpu.VMEM)
    landing = pltpu.VMEM((chips, heads, columns, tokens), jnp.bfloat16)
    crossing = pltpu.VMEM((head_groups, heads, columns, rows), jnp.bfloat16)
    counts = (chips, chips, chips, chips, head_groups, head_groups)
    return pl.pallas_call(
        functools.partial(exchange_kernel, groups, head_groups),
        in_specs=[vmem],
        out_specs=vmem,
        out_shape=jax.ShapeDtypeStruct((head_groups * heads, columns, rows), jnp.float32),
        scratch_shapes=[landing, landing, landing, crossing, crossing]
        + [pltpu.SemaphoreType.DMA((n,)) for n in counts],
        compiler_params=pltpu.CompilerParams(
            collective_id=1, has_side_effects=True, vmem_limit_bytes=VMEM_LIMIT
        ),
        name="exchange_bias",
    )(parts)


def per_device(
    groups,
    head_groups,
    input_tokens,
    output_cotangent,
    query_weight,
    key_weight,
    value_weight,
    output_weight,
    pair_bias,
    valid_len,
    pair_in,
    w_bias,
    t_gate,
    t_up,
    t_down,
):
    tokens = input_tokens.shape[1]
    token_terms, bias_parts = attention(
        input_tokens,
        output_cotangent,
        query_weight,
        key_weight,
        value_weight,
        output_weight,
        pair_bias,
        valid_len,
    )
    d_tokens = lax.psum_scatter(token_terms, "head", scatter_dimension=1, tiled=True)
    d_tokens = d_tokens.transpose(0, 2, 1)
    owned_grad = exchange_bias(bias_parts, groups, head_groups)
    d_pair, sums = pair_transitions(pair_in, owned_grad, w_bias, t_gate, t_up, t_down)
    totals = sum_everywhere(sums, groups, head_groups, tokens)
    layers, _, hidden = t_gate.shape
    totals = totals.reshape(3, layers, pair_in.shape[2], hidden)
    return (
        d_tokens,
        d_pair,
        totals[0],
        totals[1],
        totals[2].transpose(0, 2, 1),
    )


def solution(mesh):
    placed = (
        P("samp", None, None),
        P("samp", None, None),
        P(None, "head"),
        P(None, "head"),
        P(None, "head"),
        P("head", None),
        P("head", None, None),
        P(),
        P("head", "samp", None),
        P(),
        P(),
        P(),
        P(),
    )
    return jax.shard_map(
        functools.partial(per_device, mesh.shape["samp"], mesh.shape["head"]),
        mesh=mesh,
        in_specs=placed,
        out_specs=(P("samp", None, "head"), P("head", "samp", None), P(), P(), P()),
        check_vma=False,
    )
```
